512 devices in a mesh: leaf: 128 (over z, y, core), rhs: 4 (over x).
Axes of the slice: x: 4, y: 8, z: 8, core: 2. Of those that a mesh axis runs over, the one named last changes fastest.
Arguments:
- right_side: bfloat16 [64, 524288], P(None, ('leaf', 'rhs')), may hold values from -6 to 6
- point_order: int32 [524288], P('leaf'), may hold values from 0 to 4095, as said below
- leaf_inverse: bfloat16 [1024, 512, 512], P('leaf', 'rhs')
- leaf_basis: bfloat16 [1024, 512, 256], P('leaf', 'rhs'), may hold values from -0.25 to 0.25
- leaf_coupling: bfloat16 [1024, 512, 256], P('leaf', 'rhs'), may hold values from -0.1875 to 0.1875
- node_inverse: bfloat16 [1024, 512, 512], P('leaf', 'rhs')
- node_basis: bfloat16 [1024, 512, 256], P('leaf', 'rhs'), may hold values from -0.25 to 0.25
- node_coupling: bfloat16 [1024, 512, 256], P('leaf', 'rhs'), may hold values from -0.375 to 0.375
Outputs:
- coefficients: float32 [1024, 64, 512], P('leaf', None, 'rhs')
The draws below stay inside these ranges and needn't reach their ends.
Inputs may be any that keep to these rules, and one draw needn't show every extreme that they name: `point_order`: within each block of 4096 entries that one index of leaf holds, every number from 0 to 4095 stands once.
All inputs are finite; a program needn't handle non-finite values.
Results may differ from the reference program's by a relative error of at most 0.03.
Values may be sent and summed in bfloat16 or wider, within the bound.
A program may use at most 64 MiB of HBM per device.

```python
import jax
import jax.numpy as jnp
import numpy as np
from jax import lax

LEAF = 512
RANK = 256
NRHS = 64
LPD = 8
NODE = 512
NL = 1024
NPOINTS = 524288
LOCAL = 3
KX = 7
N_LEAF = 128


def with_diagonal(diag_key, off_values, size):
    diagonal = jnp.exp(jax.random.uniform(diag_key, off_values.shape[:2], jnp.float32, jnp.log(0.4), jnp.log(1.6)))
    identity = jnp.eye(size, dtype=jnp.float32)
    return off_values * (1.0 - identity) + identity * diagonal[:, :, None]


def group_order(group_key):
    return jax.random.permutation(group_key, LPD * LEAF)


def draw_point_order(key, part):
    key = jax.random.fold_in(key, 1)
    group_keys = jax.random.split(key, NL // LPD)
    orders = jax.vmap(group_order)(group_keys)
    return orders.reshape(-1).astype(jnp.int32)


def draw_leaf_inverse(key, part):
    key = jax.random.fold_in(key, 2)
    diag_key, off_key = jax.random.split(key)
    off_values = 0.4 * jax.random.truncated_normal(off_key, -4.0, 4.0, (NL, LEAF, LEAF), jnp.float32) / LEAF ** 0.5
    return with_diagonal(diag_key, off_values, LEAF).astype(jnp.bfloat16)


def draw_node_inverse(key, part):
    key = jax.random.fold_in(key, 3)
    diag_key, off_key = jax.random.split(key)
    off_values = 0.4 * jax.random.truncated_normal(off_key, -4.0, 4.0, (NL, NODE, NODE), jnp.float32) / NODE ** 0.5
    return with_diagonal(diag_key, off_values, NODE).astype(jnp.bfloat16)


def block_scale(rng, dims, pieces, least, largest):
    gain = 1.0
    for dim, shards_of in pieces:
        steps = jax.random.uniform(jax.random.fold_in(jax.random.fold_in(rng, 6), dim), (shards_of,), jnp.float32, least / len(pieces), largest / len(pieces))
        gain = gain * jnp.repeat(jnp.exp(steps), dims[dim] // shards_of).reshape((-1,) + (1,) * (len(dims) - 1 - dim))
    return gain


def normal_values(key, shape, width, most, cuts=(), kind=jnp.bfloat16):
    result = width * jax.random.normal(key, shape, jnp.float32)
    if cuts:
        result = result * block_scale(key, shape, cuts, -0.22, 0.18)
    return jnp.clip(result, -most, most).astype(kind)


def setup_inputs(seed: int = 0) -> dict:
    key_list = jax.random.split(jax.random.key(seed), 9)
    return {
        "right_side": normal_values(key_list[0], (NRHS, NPOINTS), 1.0, 6.0, ((1, 512),)),
        "point_order": draw_point_order(jax.random.fold_in(key_list[8], 71), 0),
        "leaf_inverse": draw_leaf_inverse(jax.random.fold_in(key_list[8], 71), 0),
        "leaf_basis": normal_values(key_list[3], (NL, LEAF, RANK), LEAF ** -0.5, 0.25, ((0, 128), (1, 4))),
        "leaf_coupling": normal_values(key_list[4], (NL, LEAF, RANK), (4 * RANK) ** -0.5, 0.1875, ((0, 128), (1, 4))),
        "node_inverse": draw_node_inverse(jax.random.fold_in(key_list[8], 71), 0),
        "node_basis": normal_values(key_list[6], (NL, NODE, RANK), NODE ** -0.5, 0.25, ((0, 128), (1, 4))),
        "node_coupling": normal_values(key_list[7], (NL, NODE, RANK), RANK ** -0.5, 0.375, ((0, 128), (1, 4))),
    }


def product(left_side, right_side_mat, form):
    return jnp.einsum(form, left_side.astype(jnp.float32), right_side_mat.astype(jnp.float32))


def rounded(values):
    return lax.optimization_barrier(values.astype(jnp.bfloat16))


def pair_up(values):
    return jnp.concatenate([values[0::2], values[1::2]], axis=-1)


def split_down(values, rank_size):
    joined = jnp.stack([values[..., :rank_size], values[..., rank_size:]], axis=1)
    return joined.reshape((-1,) + values.shape[1:-1] + (rank_size,))


def owner_list(height):
    return (2 * np.arange(N_LEAF >> height) + 1) * (1 << (height - 1))


def group_up(arguments):
    ordered, inverse, basis, node_inv, node_bas = arguments
    leaf_values = product(ordered, inverse, "lsj,lij->lsi")
    compressed = product(rounded(leaf_values), basis, "lsi,lik->lsk").astype(jnp.bfloat16)
    solved_all = []
    for height in range(1, LOCAL + 1):
        node_count = LPD >> height
        offset = LPD - 2 * node_count
        solved = product(pair_up(compressed), node_inv[offset:offset + node_count], "nsj,nij->nsi")
        solved_all.append(solved)
        compressed = product(rounded(solved), node_bas[offset:offset + node_count], "nsi,nik->nsk").astype(jnp.bfloat16)
    return leaf_values, compressed[0], solved_all


def group_down(arguments):
    incoming, solved_all, node_cou, leaf_values, coupling = arguments
    current = incoming[None]
    for height in range(LOCAL, 0, -1):
        node_count = LPD >> height
        offset = LPD - 2 * node_count
        node_value = solved_all[height - 1] - product(current, node_cou[offset:offset + node_count], "nsk,nik->nsi")
        current = split_down(node_value.astype(jnp.bfloat16), RANK)
    return leaf_values - product(current, coupling, "lsk,lik->lsi")


def reference(right_side, point_order, leaf_inverse, leaf_basis, leaf_coupling, node_inverse, node_basis, node_coupling):
    blocks = right_side.reshape(NRHS, N_LEAF, LPD * LEAF)
    order_rows = jnp.broadcast_to(point_order.reshape(1, N_LEAF, LPD * LEAF), blocks.shape)
    ordered = jnp.take_along_axis(blocks, order_rows, axis=2)
    ordered = ordered.reshape(NRHS, N_LEAF, LPD, LEAF).transpose(1, 2, 0, 3)
    node_inv = node_inverse.reshape(N_LEAF, LPD, NODE, NODE)
    node_bas = node_basis.reshape(N_LEAF, LPD, NODE, RANK)
    node_cou = node_coupling.reshape(N_LEAF, LPD, NODE, RANK)
    leaf_values, compressed, solved_all = lax.map(group_up, (
        ordered,
        leaf_inverse.reshape(N_LEAF, LPD, LEAF, LEAF),
        leaf_basis.reshape(N_LEAF, LPD, LEAF, RANK),
        node_inv, node_bas))
    cross_inv = node_inv[:, LPD - 1]
    cross_bas = node_bas[:, LPD - 1]
    cross_cou = node_cou[:, LPD - 1]
    cross_solved = []
    for height in range(1, KX + 1):
        owners = owner_list(height)
        solved = product(pair_up(compressed), cross_inv[owners], "nsj,nij->nsi")
        cross_solved.append(solved)
        if height < KX:
            compressed = product(rounded(solved), cross_bas[owners], "nsi,nik->nsk").astype(jnp.bfloat16)
    node_value = cross_solved[KX - 1]
    incoming = split_down(node_value.astype(jnp.bfloat16), RANK)
    for height in range(KX, 0, -1):
        incoming = split_down(node_value.astype(jnp.bfloat16), RANK)
        if height > 1:
            owners = owner_list(height - 1)
            node_value = cross_solved[height - 2] - product(incoming, cross_cou[owners], "nsk,nik->nsi")
    coefficients = lax.map(group_down, (
        incoming, solved_all, node_cou, leaf_values,
        leaf_coupling.reshape(N_LEAF, LPD, LEAF, RANK)))
    return coefficients.reshape(NL, NRHS, LEAF)
```

```python
import jax
import jax.numpy as jnp
from jax import lax
from jax.experimental import pallas as pl
from jax.experimental.pallas import tpu as pltpu
from jax.sharding import PartitionSpec as P

MESH = pl.DeviceIdType.MESH
BF = jnp.bfloat16
F32 = jnp.float32
VMEM = pltpu.VMEM


def nt(a, b):
    return lax.dot_general(a, b, (((1,), (1,)), ((), ())), preferred_element_type=F32)


def nn(a, b):
    return lax.dot_general(a, b, (((1,), (0,)), ((), ())), preferred_element_type=F32)


def xor(a, k):
    total = 0
    for bit in (1, 2):
        digit = (a // bit) % 2
        total = total + bit * ((1 - digit) if k & bit else digit)
    return total


def when(cond):
    return pl.when(cond)


N_SEMS = 96


def kernel(
    rs, po, linv, lbas, lcou, ninv, nbas, ncou, out,
    tg, acc, lv, linv_v, lbas_v, lcou_v, ninv_v, nbas_v, ncou_v,
    rsb, rsr, c0g, p1, p1r, c1, p2, p2r, c2, p3, p3r, c3, c3l,
    s1, s2, s3, finv, fbas, fcou, fs, cs, up2, up3, up4, up5, up6, up7,
    vb, db, incg, d3, d2, d1,
    lsem, ssem, rsem, fss, frs,
):
    leaf = lax.axis_index("leaf")
    x = lax.axis_index("rhs")
    core = leaf % 2
    y = (leaf // 2) % 8
    z = leaf // 16

    def at(z_, y_, c_, x_):
        return ((z_ * 8 + y_) * 2 + c_, x_)

    counter = [0]
    pending = []

    def remote(src, dst, target, my_dst=None, cond=None, lands=None):
        i = counter[0]
        counter[0] += 1
        j = i if lands is None else lands
        send = pltpu.make_async_remote_copy(
            src_ref=src, dst_ref=dst, send_sem=ssem.at[i], recv_sem=rsem.at[j],
            device_id=target, device_id_type=MESH,
        )
        here = dst if my_dst is None else my_dst
        recv = pltpu.make_async_remote_copy(
            src_ref=src, dst_ref=here, send_sem=ssem.at[i], recv_sem=rsem.at[j],
            device_id=target, device_id_type=MESH,
        )
        pending.append((cond, send))
        return send, recv

    local = [
        pltpu.make_async_copy(src, dst, lsem.at[i])
        for i, (src, dst) in enumerate(
            (
                (linv, linv_v), (lbas, lbas_v),
                (ninv.at[pl.ds(0, 7)], ninv_v), (nbas.at[pl.ds(0, 7)], nbas_v),
                (ncou.at[pl.ds(0, 7)], ncou_v), (lcou, lcou_v),
            )
        )
    ]
    for copy in local:
        copy.start()

    xs = [xor(x, k) for k in range(4)]
    is0 = core == 0
    is1 = core == 1
    y_odd = y % 2 == 1
    y_mid = y % 4 == 2
    z_odd = z % 2 == 1
    z_mid = z % 4 == 2
    y_pair = y + 1 - 2 * (y % 2)
    z_pair = z + 1 - 2 * (z % 2)
    y_own = (y // 4) * 4 + 2
    z_own = (z // 4) * 4 + 2
    row1 = is1 & (y == 0)
    moved = is0 & (y == 4)
    y_to = jnp.where(moved, 0, y)

    barrier = pltpu.get_barrier_semaphore()

    def greet(*target):
        pl.semaphore_signal(barrier, inc=1, device_id=at(*target), device_id_type=MESH)

    def greet_if(cond, *targets):
        @when(cond)
        def _():
            for target in targets:
                greet(*target)

    def as_int(cond):
        return jnp.where(cond, 1, 0)

    for k in (1, 2, 3):
        greet(z, y, core, xs[k])
    greet(z, y, 1 - core, x)
    greet_if(is1 & (y != 4), *[(z, y, 0, xs[k]) for k in (1, 2, 3)])
    greet_if(row1, *[(z, 4, 0, xs[k]) for k in range(4)])
    greet_if(is1, (z, y_pair, 1, x))
    greet_if(is1 & y_odd, (z, y_own, 1, x))
    greet_if(is1 & y_mid, (z, y - 1, 1, x), (z, y + 1, 1, x), (z, 0, 1, x))
    greet_if(row1, (z, 2, 1, x), (z, 6, 1, x), (z_pair, 0, 1, x))
    greet_if(row1 & z_odd, (z_own, 0, 1, x))
    greet_if(row1 & z_mid, (z - 1, 0, 1, x), (z + 1, 0, 1, x), (4, 0, 1, x))
    greet_if(row1 & (z == 4), (2, 0, 1, x), (6, 0, 1, x))
    expect = (
        4
        + as_int(is0) * 3
        + as_int(moved)
        + as_int(is1)
        + as_int(is1 & y_odd)
        + as_int(is1 & y_mid) * 3
        + as_int(row1) * 3
        + as_int(row1 & z_odd)
        + as_int(row1 & z_mid) * 3
        + as_int(row1 & (z == 4)) * 2
    )
    pl.semaphore_wait(barrier, expect)

    gather = [
        remote(rs, tg.at[k - 1], at(z, y, core, xs[k])) for k in (1, 3, 2)
    ]
    for send, _ in gather:
        send.start()

    slot = jnp.where(is1, 0, jnp.where(moved, 2, 1))
    factors = ((ninv.at[7], finv), (nbas.at[7], fbas), (ncou.at[7], fcou))

    def factor_copy(which, k):
        src, dst = factors[which]
        return pltpu.make_async_remote_copy(
            src_ref=src, dst_ref=dst.at[slot, x], send_sem=fss.at[which, k],
            recv_sem=frs.at[which, slot, k], device_id=at(z, y_to, 1, xs[k]), device_id_type=MESH,
        )

    def factor_own(which):
        src, dst = factors[which]
        return pltpu.make_async_copy(src, dst.at[0, x], fss.at[which, 0])

    def send_factors(which):
        for k in (1, 3, 2):
            factor_copy(which, k).start()

        @when(is0)
        def _():
            factor_copy(which, 0).start()

        @when(is1)
        def _():
            factor_own(which).start()

    def wait_factors(which, place):
        src, dst = factors[which]
        for k in range(4):
            if place == 0 and k == 0:
                factor_own(which).wait()
                continue
            pltpu.make_async_remote_copy(
                src_ref=src, dst_ref=dst.at[place, xs[k]], send_sem=fss.at[which, k],
                recv_sem=frs.at[which, place, k], device_id=at(z, y, 0, xs[k]), device_id_type=MESH,
            ).wait_recv()

    wide = 512

    def permute(block, source, first):
        base = source * 1024

        def part(j, carry):
            cols = pl.ds(pl.multiple_of(j * wide, wide), wide)
            rows = lax.broadcasted_iota(jnp.int32, (1024, wide), 0) + base
            hot = jnp.where(rows == po[:, cols], 1.0, 0.0).astype(BF)
            term = nn(block, hot)
            acc[:, cols] = term if first else acc[:, cols] + term
            return carry

        lax.fori_loop(0, 4096 // wide, part, 0)

    permute(rs[...], x, True)
    for (_, recv), k in zip(gather, (1, 3, 2)):
        recv.wait_recv()
        permute(tg[k - 1], xs[k], False)

    local[0].wait()
    local[1].wait()
    for l in range(8):
        value = nt(acc[:, l * 512 : (l + 1) * 512].astype(BF), linv_v[l])
        lv[l] = value
        part = nn(value.astype(BF), lbas_v[l]).astype(BF)
        for q in range(4):
            rsb[q, l] = part[16 * q : 16 * q + 16]

    scatter = [remote(rsb.at[xs[k]], rsr.at[k - 1], at(z, y, core, xs[k])) for k in (1, 3, 2)]
    for send, _ in scatter:
        send.start()
    send_factors(0)
    for _, recv in scatter:
        recv.wait_recv()
    total = rsb[x].astype(F32)
    for k in range(3):
        total = total + rsr[k].astype(F32)
    c0g[x] = total.astype(BF)

    def spread(buffer):
        copies = [
            remote(buffer.at[x], buffer.at[x], at(z, y, core, xs[k]), my_dst=buffer.at[xs[k]])
            for k in (1, 3, 2)
        ]
        for send, _ in copies:
            send.start()
        return [recv for _, recv in copies]

    for recv in spread(c0g):
        recv.wait_recv()

    local[2].wait()
    local[3].wait()

    def exchange(src, dst):
        copies = [remote(src, dst.at[k - 1], at(z, y, core, xs[k])) for k in (1, 3, 2)]
        for send, _ in copies:
            send.start()
        return [recv for _, recv in copies]

    for n in range(4):
        left = c0g[:, 2 * n].reshape(64, 256)
        right = c0g[:, 2 * n + 1].reshape(64, 256)
        solved = nt(jnp.concatenate([left, right], axis=1), ninv_v[n])
        s1[n] = solved
        p1[n] = nn(solved.astype(BF), nbas_v[n]).astype(BF)
    recvs = exchange(p1, p1r)
    send_factors(1)
    for recv in recvs:
        recv.wait_recv()
    for n in range(4):
        total = p1[n].astype(F32)
        for k in range(3):
            total = total + p1r[k, n].astype(F32)
        c1[n] = total.astype(BF)

    for n in range(2):
        solved = nt(jnp.concatenate([c1[2 * n], c1[2 * n + 1]], axis=1), ninv_v[4 + n])
        s2[n] = solved
        p2[n] = nn(solved.astype(BF), nbas_v[4 + n]).astype(BF)
    recvs = exchange(p2, p2r)
    send_factors(2)
    for recv in recvs:
        recv.wait_recv()
    for n in range(2):
        total = p2[n].astype(F32)
        for k in range(3):
            total = total + p2r[k, n].astype(F32)
        c2[n] = total.astype(BF)

    solved = nt(jnp.concatenate([c2[0], c2[1]], axis=1), ninv_v[6])
    s3[...] = solved
    part = nn(solved.astype(BF), nbas_v[6]).astype(BF)
    for q in range(4):
        p3[q] = part[16 * q : 16 * q + 16]
    scatter = [remote(p3.at[xs[k]], p3r.at[k - 1], at(z, y, core, xs[k])) for k in (1, 3, 2)]
    for send, _ in scatter:
        send.start()
    for _, recv in scatter:
        recv.wait_recv()
    total = p3[x].astype(F32)
    for k in range(3):
        total = total + p3r[k].astype(F32)
    c3[...] = total.astype(BF)

    def up(place, left, right):
        wait_factors(0, place)
        wait_factors(1, place)
        solved = nt(jnp.concatenate([left, right], axis=1), finv[place].reshape(512, 512))
        fs[place] = solved
        return nn(solved.astype(BF), fbas[place].reshape(512, 256)).astype(BF)

    def down(place, h):
        wait_factors(2, place)
        value = (fs[place] - nt(db[h], fcou[place].reshape(512, 256))).astype(BF)
        vb[h, 0] = value[:, :256]
        vb[h, 1] = value[:, 256:]

    core_up, core_up_recv = remote(c3, c3l, at(z, y, 1, x), cond=is0)
    core_down, core_down_recv = remote(vb.at[1, 0], db.at[0], at(z, y, 0, x), cond=is1)
    y_even = is1 & (y % 2 == 0)
    row_even = row1 & (z % 2 == 0)
    odd1 = is1 & y_odd
    mid1 = is1 & y_mid
    rodd = row1 & z_odd
    rmid = row1 & z_mid
    top = row1 & (z == 4)
    up2c = remote(cs.at[1], up2, at(z, y_pair, 1, x), cond=y_even)
    side3 = as_int(y % 4 == 3)
    up3c = [remote(cs.at[2], up3.at[i], at(z, y_own, 1, x), cond=odd1 & (side3 == i)) for i in (0, 1)]
    side4 = y // 4
    up4c = [remote(cs.at[3], up4.at[i], at(z, 0, 1, x), cond=mid1 & (side4 == i)) for i in (0, 1)]
    up5c = remote(cs.at[4], up5, at(z_pair, 0, 1, x), cond=row_even)
    side6 = as_int(z % 4 == 3)
    up6c = [remote(cs.at[5], up6.at[i], at(z_own, 0, 1, x), cond=rodd & (side6 == i)) for i in (0, 1)]
    side7 = z // 4
    up7c = [remote(cs.at[6], up7.at[i], at(4, 0, 1, x), cond=rmid & (side7 == i)) for i in (0, 1)]
    to = counter[0]
    dn6 = [
        remote(vb.at[7, i], db.at[6], at(2 + 4 * i, 0, 1, x), cond=top, lands=to)
        for i in (0, 1)
    ]
    to = counter[0]
    dn5 = [
        remote(vb.at[6, i], db.at[5], at(z - 1 + 2 * i, 0, 1, x), cond=rmid, lands=to)
        for i in (0, 1)
    ]
    dn4 = remote(vb.at[5, 0], db.at[4], at(z - 1, 0, 1, x), cond=rodd)
    to = counter[0]
    dn3 = [
        remote(vb.at[4, i], db.at[3], at(z, 2 + 4 * i, 1, x), cond=row1, lands=to)
        for i in (0, 1)
    ]
    to = counter[0]
    dn2 = [
        remote(vb.at[3, i], db.at[2], at(z, y - 1 + 2 * i, 1, x), cond=mid1, lands=to)
        for i in (0, 1)
    ]
    dn1 = remote(vb.at[2, 0], db.at[1], at(z, y - 1, 1, x), cond=odd1)

    def each(side, copies, act):
        for i in (0, 1):
            @when(side == i)
            def _(i=i):
                act(copies[i])

    @when(is0)
    def _():
        core_up.start()

    @when(is1)
    def _():
        core_up_recv.wait_recv()
        cs[1] = up(0, c3l[...], c3[...])

    @when(y_even)
    def _():
        up2c[0].start()

    @when(odd1)
    def _():
        up2c[1].wait_recv()
        cs[2] = up(1, up2[...], cs[1])
        each(side3, up3c, lambda c: c[0].start())

    @when(mid1)
    def _():
        up3c[0][1].wait_recv()
        up3c[1][1].wait_recv()
        cs[3] = up(1, up3[0], up3[1])
        each(side4, up4c, lambda c: c[0].start())

    @when(row1)
    def _():
        up4c[0][1].wait_recv()
        up4c[1][1].wait_recv()
        cs[4] = up(2, up4[0], up4[1])

        @when(z % 2 == 0)
        def _():
            up5c[0].start()

        @when(z_odd)
        def _():
            up5c[1].wait_recv()
            cs[5] = up(1, up5[...], cs[4])
            each(side6, up6c, lambda c: c[0].start())

        @when(z_mid)
        def _():
            up6c[0][1].wait_recv()
            up6c[1][1].wait_recv()
            cs[6] = up(1, up6[0], up6[1])
            each(side7, up7c, lambda c: c[0].start())

        @when(z == 4)
        def _():
            up7c[0][1].wait_recv()
            up7c[1][1].wait_recv()
            wait_factors(0, 1)
            value = nt(jnp.concatenate([up7[0], up7[1]], axis=1), finv[1].reshape(512, 512)).astype(BF)
            vb[7, 0] = value[:, :256]
            vb[7, 1] = value[:, 256:]
            dn6[0][0].start()
            dn6[1][0].start()
            wait_factors(1, 1)
            wait_factors(2, 1)

        @when(z_mid)
        def _():
            dn6[0][1].wait_recv()
            down(1, 6)
            dn5[0][0].start()
            dn5[1][0].start()

        @when(z_odd)
        def _():
            dn5[0][1].wait_recv()
            down(1, 5)
            dn4[0].start()
            db[4] = vb[5, 1]

        @when(z % 2 == 0)
        def _():
            dn4[1].wait_recv()

        @when(z == 0)
        def _():
            for which in range(3):
                wait_factors(which, 1)

        down(2, 4)
        dn3[0][0].start()
        dn3[1][0].start()

    @when(mid1)
    def _():
        dn3[0][1].wait_recv()
        down(1, 3)
        dn2[0][0].start()
        dn2[1][0].start()

    @when(odd1)
    def _():
        dn2[0][1].wait_recv()
        down(1, 2)
        dn1[0].start()
        db[1] = vb[2, 1]

    @when(y_even)
    def _():
        dn1[1].wait_recv()

    @when(is1)
    def _():
        down(0, 1)
        core_down.start()
        db[0] = vb[1, 1]

    @when(is0)
    def _():
        core_down_recv.wait_recv()

    incg[x] = db[0]
    for recv in spread(incg):
        recv.wait_recv()
    for i in (4, 5):
        local[i].wait()
    inc = incg[...].reshape(64, 256)
    d3[x] = (s3[...] - nt(inc, ncou_v[6])).astype(BF)
    for recv in spread(d3):
        recv.wait_recv()
    for n in range(2):
        inc = jnp.concatenate([d3[2 * n], d3[2 * n + 1]], axis=1)
        d2[x, n] = (s2[n] - nt(inc, ncou_v[4 + n])).astype(BF)
    for recv in spread(d2):
        recv.wait_recv()
    for n in range(4):
        half = 2 * (n % 2)
        inc = jnp.concatenate([d2[half, n // 2], d2[half + 1, n // 2]], axis=1)
        d1[x, n] = (s1[n] - nt(inc, ncou_v[n])).astype(BF)
    for recv in spread(d1):
        recv.wait_recv()
    for l in range(8):
        half = 2 * (l % 2)
        inc = jnp.concatenate([d1[half, l // 2], d1[half + 1, l // 2]], axis=1)
        out[l] = lv[l] - nt(inc, lcou_v[l])

    def finish(cond, copy):
        if cond is None:
            copy.wait_send()
        else:
            @when(cond)
            def _():
                copy.wait_send()

    for cond, copy in pending:
        finish(cond, copy)
    for which in range(3):
        for k in (1, 2, 3):
            factor_copy(which, k).wait_send()

        @when(is0)
        def _(which=which):
            factor_copy(which, 0).wait_send()


def body(rs, po, linv, lbas, lcou, ninv, nbas, ncou):
    vm = pl.BlockSpec(memory_space=pltpu.VMEM)
    hbm = pl.BlockSpec(memory_space=pl.ANY)
    dma = pltpu.SemaphoreType.DMA
    scratch = [
        VMEM((3, 64, 1024), BF), VMEM((64, 4096), F32), VMEM((8, 64, 128), F32),
        VMEM((8, 128, 512), BF), VMEM((8, 128, 256), BF), VMEM((8, 128, 256), BF),
        VMEM((7, 128, 512), BF), VMEM((7, 128, 256), BF), VMEM((7, 128, 256), BF),
        VMEM((4, 8, 16, 256), BF), VMEM((3, 8, 16, 256), BF), VMEM((4, 8, 16, 256), BF),
        VMEM((4, 64, 256), BF), VMEM((3, 4, 64, 256), BF), VMEM((4, 64, 256), BF),
        VMEM((2, 64, 256), BF), VMEM((3, 2, 64, 256), BF), VMEM((2, 64, 256), BF),
        VMEM((4, 16, 256), BF), VMEM((3, 16, 256), BF), VMEM((16, 256), BF), VMEM((16, 256), BF),
        VMEM((4, 64, 128), F32), VMEM((2, 64, 128), F32), VMEM((64, 128), F32),
        VMEM((3, 4, 128, 512), BF), VMEM((3, 4, 128, 256), BF), VMEM((3, 4, 128, 256), BF),
        VMEM((3, 16, 512), F32), VMEM((7, 16, 256), BF),
        VMEM((16, 256), BF), VMEM((2, 16, 256), BF), VMEM((2, 16, 256), BF),
        VMEM((16, 256), BF), VMEM((2, 16, 256), BF), VMEM((2, 16, 256), BF),
        VMEM((8, 2, 16, 256), BF), VMEM((7, 16, 256), BF), VMEM((4, 16, 256), BF),
        VMEM((4, 64, 128), BF), VMEM((4, 2, 64, 128), BF), VMEM((4, 4, 64, 128), BF),
        dma((6,)), dma((N_SEMS,)), dma((N_SEMS,)), dma((3, 4)), dma((3, 3, 4)),
    ]
    return pl.pallas_call(
        kernel,
        out_shape=jax.ShapeDtypeStruct((8, 64, 128), F32),
        in_specs=[vm, vm] + [hbm] * 6,
        out_specs=vm,
        scratch_shapes=scratch,
        compiler_params=pltpu.CompilerParams(
            collective_id=0, has_side_effects=True, vmem_limit_bytes=60 << 20
        ),
    )(rs, po.reshape(1, 4096), linv, lbas, lcou, ninv, nbas, ncou)


def solution(mesh):
    placed = (
        P(None, ("leaf", "rhs")),
        P("leaf"),
        P("leaf", "rhs", None),
        P("leaf", "rhs", None),
        P("leaf", "rhs", None),
        P("leaf", "rhs", None),
        P("leaf", "rhs", None),
        P("leaf", "rhs", None),
    )
    return jax.shard_map(
        body, mesh=mesh, in_specs=placed, out_specs=P("leaf", None, "rhs"), check_vma=False
    )
```

```python
import jax
import jax.numpy as jnp
from jax import lax
from jax.experimental import pallas as pl
from jax.experimental.pallas import tpu as pltpu
from jax.sharding import PartitionSpec as P

MESH = pl.DeviceIdType.MESH
BF = jnp.bfloat16
F32 = jnp.float32
VMEM = pltpu.VMEM
HOME = 1
HIGH = 2
N_SEMS = 128
ALONG_X = (1, 3, 2)
WHEN = {0: (), 1: ("fi", "fb", "n1i", "n1b"), 2: (), 3: (), 4: ("n2i", "n2b", "pi", "pb"), 5: (), 6: ("fc",), 7: ("c1", "pc")}


def nt(a, b):
    return lax.dot_general(a, b, (((1,), (1,)), ((), ())), preferred_element_type=F32)


def nn(a, b):
    return lax.dot_general(a, b, (((1,), (0,)), ((), ())), preferred_element_type=F32)


def xor(a, k):
    total = 0
    for bit in (1, 2):
        digit = (a // bit) % 2
        total = total + bit * ((1 - digit) if k & bit else digit)
    return total


def as_int(cond):
    return jnp.where(cond, 1, 0)


def kernel(
    rs, po, linv, lbas, lcou, ninv, nbas, ncou, out,
    tg, acc, lv, linv_v, lbas_v, lcou_v, rsb, rsr,
    n1i, n1b, n1c, n2i, n2b, c2h, c3h,
    s1, s2b, s3b, s2h, s3h, cb1, u2x, cb2, u3x,
    finv, fbas, fcou, fs1, fsv, fsz, cs, u1, u2, u34, u5, u67,
    sh2, sh5, sb2, sb5, id2, id5, vy, vz, vcore, inc3, i0,
    lsem, ssem, rsem, fss, frs,
):
    leaf = lax.axis_index("leaf")
    x = lax.axis_index("rhs")
    core = leaf % 2
    y = (leaf // 2) % 8
    z = leaf // 16

    def at(z_, y_, c_, x_):
        return ((z_ * 8 + y_) * 2 + c_, x_)

    counter = [0]
    pending = []

    def remote(src, dst, target, my_dst=None, cond=None, lands=None):
        i = counter[0]
        counter[0] += 1
        j = i if lands is None else lands
        made = [
            pltpu.make_async_remote_copy(
                src_ref=src, dst_ref=here, send_sem=ssem.at[i], recv_sem=rsem.at[j],
                device_id=target, device_id_type=MESH,
            )
            for here in (dst, dst if my_dst is None else my_dst)
        ]
        pending.append((cond, made[0]))
        return made

    def begin(copy, cond=None):
        if cond is None:
            copy.start()
        else:
            @pl.when(cond)
            def _():
                copy.start()

    local_count = [0]

    def local(src, dst):
        i = local_count[0]
        local_count[0] += 1
        return pltpu.make_async_copy(src, dst, lsem.at[i])

    xs = [xor(x, k) for k in range(4)]
    is0 = core == 0
    is1 = core == 1
    y_odd = y % 2 == 1
    z_odd = z % 2 == 1
    y_pair = y + 1 - 2 * (y % 2)
    z_pair = z + 1 - 2 * (z % 2)
    home = x == HOME
    plane = is1 & home
    high = is1 & (x == HIGH)
    spine = high & (y == 0)
    top = spine & (z == 4)
    low = x < 2

    own_linv, own_lbas, own_lcou = (
        local(linv, linv_v), local(lbas, lbas_v), local(lcou, lcou_v)
    )
    own_n1 = [local(a.at[x], b.at[x]) for a, b in ((ninv, n1i), (nbas, n1b), (ncou, n1c))]
    for copy in [own_linv, own_lbas, own_lcou] + own_n1:
        copy.start()

    def entry(at_x):
        return 4 + as_int(at_x == 1) * 2 + as_int(at_x == 2)

    has_n2 = x != 3
    own_entry = jnp.where(has_n2, entry(x), 4)
    own_n2 = [local(a.at[own_entry], b.at[x]) for a, b in ((ninv, n2i), (nbas, n2b))]
    for copy in own_n2:
        copy.start()

    barrier = pltpu.get_barrier_semaphore()

    def greet(*target):
        pl.semaphore_signal(barrier, inc=1, device_id=at(*target), device_id_type=MESH)

    def greet_if(cond, *targets):
        @pl.when(cond)
        def _():
            for target in targets:
                greet(*target)

    for k in ALONG_X:
        greet(z, y, core, xs[k])
    greet(z, y, 1 - core, x)
    odds = (1, 3, 5, 7)
    y_even = y % 2 == 0
    z_even = z % 2 == 0
    greet_if(plane & y_odd, *[(z, y, 0, r) for r in (2, 3)])
    greet_if(plane & y_even, *[(z, y + 1, 0, r) for r in (0, 1)])
    greet_if(plane, (z, y + as_int(y_even), 1, HIGH), (z, 0, 1, HIGH))
    greet_if(high & y_odd, *[(z, y, 0, r) for r in range(4)])
    greet_if(high & y_odd, (z, y, 1, HOME), (z, y - 1, 1, HOME))
    greet_if(high & y_even & (y > 0), *[(z, y, 0, r) for r in range(4)])
    greet_if(spine, *[(z, t, 1, HIGH) for t in range(1, 8)])
    greet_if(spine, (z_pair, 0, 1, HIGH))
    greet_if(spine & (z > 0), *[(z, 0, 0, r) for r in range(4)])
    greet_if(spine & z_even, *[(z + 1, 0, 0, r) for r in (0, 1)])
    greet_if(spine & (z != 4), (4, 0, 1, HIGH))
    greet_if(top, *[(t, 0, 1, HIGH) for t in (1, 2, 3, 5, 6, 7)])
    mover = jnp.where(y > 0, 1 + as_int(y_odd), as_int(z > 0) + as_int(z_odd & low))
    expect = (
        4
        + as_int(is0) * mover
        + as_int(plane)
        + as_int(high & y_odd) * 3
        + as_int(high & y_even & (y > 0))
        + as_int(spine) * (9 + as_int(z_odd) + as_int(z % 4 == 2))
        + as_int(top) * 7
    )
    pl.semaphore_wait(barrier, expect)

    gather = {k: remote(rs, tg.at[k - 1], at(z, y, core, xs[k])) for k in ALONG_X}
    gather[1][0].start()
    gather[3][0].start()

    def along_x(src, dst, k, cond=None):
        return remote(src, dst.at[x], at(z, y, core, xs[k]), my_dst=dst.at[xs[k]], cond=cond)

    move_n1 = [along_x(a.at[xs[k]], b, k) for a, b in ((ninv, n1i), (nbas, n1b)) for k in ALONG_X]
    move_c1 = [along_x(ncou.at[xs[k]], n1c, k) for k in ALONG_X]
    goes_n2 = {k: xs[k] != 3 for k in ALONG_X}
    move_n2 = [
        along_x(a.at[jnp.where(goes_n2[k], entry(xs[k]), 4)], b, k, cond=goes_n2[k])
        for a, b in ((ninv, n2i), (nbas, n2b))
        for k in ALONG_X
    ]

    first_row = is0 & (y == 0)
    slot = jnp.where(
        is1,
        0,
        jnp.where(
            y > 0,
            jnp.where(y_odd, 1, jnp.where(y == 2, 2, jnp.where(y == 6, 3, 4))),
            jnp.where(z_odd, 1, jnp.where(z == 2, 5, jnp.where(z == 6, 6, 7))),
        ),
    )
    halved_y = is0 & y_odd
    halved_z = first_row & z_odd
    slot_c = jnp.where(halved_y, 8, jnp.where(halved_z, 9, slot))
    to_y_c = y - as_int(halved_y & low)
    to_z_c = z - as_int(halved_z & low)
    stays = plane
    to_x = jnp.where(is1, HOME, HIGH)
    to_x_c = jnp.where(halved_y, HOME, to_x)
    has_inv = jnp.logical_not(first_row & (z == 0)) & jnp.logical_not(stays)
    has_rest = has_inv & jnp.logical_not(first_row & (z == 4))
    factors = ((ninv.at[7], finv), (nbas.at[7], fbas), (ncou.at[7], fcou))

    def factor_copy(which):
        src, dst = factors[which]
        place = slot_c if which == 2 else slot
        target = at(to_z_c, to_y_c, 1, to_x_c) if which == 2 else at(z, y, 1, to_x)
        return pltpu.make_async_remote_copy(
            src_ref=src, dst_ref=dst.at[place, x], send_sem=fss.at[which],
            recv_sem=frs.at[which, place, x], device_id=target, device_id_type=MESH,
        )

    def factor_own(which):
        src, dst = factors[which]
        return pltpu.make_async_copy(src, dst.at[0, HOME], fss.at[which])

    def send_factors(which):
        begin(factor_copy(which), has_inv if which == 0 else has_rest)
        begin(factor_own(which), stays)

    def wait_factor(which, place, r):
        src, dst = factors[which]
        pltpu.make_async_remote_copy(
            src_ref=src, dst_ref=dst.at[place, r], send_sem=fss.at[which],
            recv_sem=frs.at[which, place, r], device_id=at(z, y, 0, x), device_id_type=MESH,
        ).wait_recv()

    def wait_factors(which, place):
        for r in range(4):
            if place == 0 and r == HOME:
                factor_own(which).wait()
            else:
                wait_factor(which, place, r)

    def start_all(moves, conds=None):
        for n, (send, _) in enumerate(moves):
            begin(send, conds[n] if conds else None)

    n2_conds = [goes_n2[k] for k in ALONG_X]
    items = {
        "n1i": lambda: start_all(move_n1[:3]),
        "n1b": lambda: start_all(move_n1[3:]),
        "n2i": lambda: start_all(move_n2[:3], n2_conds),
        "n2b": lambda: start_all(move_n2[3:], n2_conds),
        "fi": lambda: send_factors(0),
        "fb": lambda: send_factors(1),
        "fc": lambda: send_factors(2),
        "c1": lambda: start_all(move_c1),
        "pi": lambda: pass_on(0),
        "pb": lambda: pass_on(1),
        "pc": lambda: pass_on(2),
    }

    def point(n):
        for item in WHEN[n]:
            items[item]()

    passing = [(2, high & (y == 2), (z, 0)), (3, high & (y == 6), (z, 0)), (4, high & (y == 4), (z, 0))]
    passing += [(5, spine & (z == 2), (4, 0)), (6, spine & (z == 6), (4, 0))]
    passed = {
        (which, place): remote(
            factors[which][1].at[place], factors[which][1].at[place], at(*to, 1, HIGH), cond=cond
        )
        for place, cond, to in passing
        for which in range(3)
    }

    def pass_on(which):
        for place, cond, _ in passing:
            @pl.when(cond)
            def _(place=place):
                wait_factors(which, place)
                passed[which, place][0].start()

    wide = 512

    def permute(block, source, first):
        base = source * 1024

        def part(j, carry):
            cols = pl.ds(pl.multiple_of(j * wide, wide), wide)
            rows = lax.broadcasted_iota(jnp.int32, (1024, wide), 0) + base
            hot = jnp.where(rows == po[:, cols], 1.0, 0.0).astype(BF)
            term = nn(block, hot)
            acc[:, cols] = term if first else acc[:, cols] + term
            return carry

        lax.fori_loop(0, 4096 // wide, part, 0)

    point(0)
    permute(rs[...], x, True)
    gather[2][0].start()
    point(1)
    gather[1][1].wait_recv()
    permute(tg[0], xs[1], False)
    point(2)
    gather[3][1].wait_recv()
    permute(tg[2], xs[3], False)
    point(3)
    gather[2][1].wait_recv()
    permute(tg[1], xs[2], False)

    own_linv.wait()
    own_lbas.wait()
    scatter = {k: remote(rsb.at[xs[k]], rsr.at[k - 1], at(z, y, core, xs[k])) for k in ALONG_X}
    for k in (2, 1, 3, 0):
        for j in range(2):
            l = 2 * xs[k] + j
            cols = pl.ds(pl.multiple_of(l * 512, 512), 512)
            value = nt(acc[:, cols].astype(BF), linv_v[l])
            lv[l] = value
            rsb[xs[k], j] = nn(value.astype(BF), lbas_v[l]).astype(BF)
        if k:
            scatter[k][0].start()
    point(4)
    for k in ALONG_X:
        scatter[k][1].wait_recv()

    def summed(j):
        total = rsb[x, j].astype(F32)
        for k in range(3):
            total = total + rsr[k, j].astype(F32)
        return total.astype(BF)

    def solve(left, right, inverse):
        return nt(jnp.concatenate([left, right], axis=1), inverse.reshape(512, 512))

    def squeeze(solved, basis):
        return nn(solved.astype(BF), basis.reshape(512, 256)).astype(BF)

    point(5)
    for _, recv in move_n1:
        recv.wait_recv()
    own_n1[0].wait()
    own_n1[1].wait()
    solved = solve(summed(0), summed(1), n1i[...])
    s1[...] = solved
    cb1[...] = squeeze(solved, n1b[...])

    x_odd = x % 2 == 1
    x_even = x % 2 == 0
    up_l1 = remote(cb1, u2x, at(z, y, core, xs[1]), cond=x_odd)
    to_home = counter[0]
    up_l2 = [
        remote(cb2, u3x.at[i], at(z, y, core, HOME), cond=x == 2 * i) for i in (0, 1)
    ]
    share_s2 = remote(s2b.at[1], s2h, at(z, y, core, xs[1]), cond=x_even)
    landing = counter[0]
    share_s3 = {
        t: remote(s3b.at[t // 2], s3h, at(z, y, core, t), cond=home, lands=landing) for t in (0, 2, 3)
    }
    begin(up_l1[0], x_odd)
    point(6)

    own_n2[0].wait()
    own_n2[1].wait()

    @pl.when(has_n2)
    def _():
        for _, recv in move_n2:
            recv.wait_recv()

    @pl.when(x_even)
    def _():
        up_l1[1].wait_recv()
        solved = solve(cb1[...], u2x[...], n2i[...])
        cb2[...] = squeeze(solved, n2b[...])
        for i in (0, 1):
            begin(up_l2[i][0], x == 2 * i)
        rounded = solved.astype(BF)
        s2b[1] = rounded[:, 256:]
        s2h[...] = rounded[:, :256]
        share_s2[0].start()

    @pl.when(home)
    def _():
        for i in (0, 1):
            up_l2[i][1].wait_recv()
        solved = solve(u3x[0], u3x[1], n2i[...])
        cb2[...] = squeeze(solved, n2b[...])
        rounded = solved.astype(BF)
        s3b[0] = rounded[:, :256]
        s3b[1] = rounded[:, 256:]

    cross_up = remote(cb2, u1, at(z, y, 1, x), cond=is0 & home)
    begin(cross_up[0], is0 & home)
    for t in (0, 2, 3):
        begin(share_s3[t][0], home)

    @pl.when(home)
    def _():
        s3h[...] = s3b[HOME // 2]

    high_odd = high & y_odd
    spine_odd = spine & z_odd
    spine_even = spine & z_even
    y_own = y + as_int(y_even)
    up2 = [
        remote(cs.at[0], u2.at[i], at(z, y_own, 1, HIGH), cond=plane & (y % 2 == i)) for i in (0, 1)
    ]
    landing = counter[0]
    share2 = [
        remote(sb2.at[i], sh2, at(z, y - 1 + i, 1, HOME), cond=high_odd, lands=landing) for i in (0, 1)
    ]
    up34 = [
        remote(cs.at[1], u34.at[m], at(z, 0, 1, x), cond=high & (y == 2 * m + 1)) for m in range(4)
    ]
    up5 = remote(cs.at[2], u5, at(z_pair, 0, 1, x), cond=spine_even)
    share5 = remote(sb5, sh5, at(z_pair, 0, 1, x), cond=spine_odd)
    up67 = [
        remote(cs.at[3], u67.at[m], at(4, 0, 1, x), cond=spine & (z == 2 * m + 1)) for m in range(4)
    ]
    landing = counter[0]
    down_z = {
        t: remote(vz.at[t // 2], id5, at(t, 0, 1, x), cond=top, lands=landing)
        for t in (0, 1, 2, 3, 5, 6, 7)
    }
    landing = counter[0]
    down_y = {
        t: remote(vy.at[t // 2], id2, at(z, t, 1, HOME), cond=spine, lands=landing) for t in range(8)
    }
    cross_down = remote(vcore, inc3, at(z, y, 0, x), cond=plane)

    @pl.when(plane)
    def _():
        wait_factors(0, 0)
        wait_factors(1, 0)
        cross_up[1].wait_recv()
        solved = solve(u1[...], cb2[...], finv[0])
        cs[0] = squeeze(solved, fbas[0])
        for i in (0, 1):
            begin(up2[i][0], y % 2 == i)
        fs1[...] = solved

    @pl.when(high_odd)
    def _():
        wait_factors(0, 1)
        wait_factors(1, 1)
        for i in (0, 1):
            up2[i][1].wait_recv()
        solved = solve(u2[0], u2[1], finv[1])
        cs[1] = squeeze(solved, fbas[1])
        for m in range(4):
            begin(up34[m][0], y == 2 * m + 1)
        rounded = solved.astype(BF)
        for i in (0, 1):
            sb2[i] = rounded[:, 256 * i : 256 * i + 256]
            share2[i][0].start()

    def pair_up(arrived, buffer, first, store):
        squeezed = []
        for i in (0, 1):
            arrived[2 * i][1].wait_recv()
            arrived[2 * i + 1][1].wait_recv()
            solved = solve(buffer[2 * i], buffer[2 * i + 1], finv[first + i])
            store[i] = solved
            squeezed.append(squeeze(solved, fbas[first + i]))
        return solve(squeezed[0], squeezed[1], finv[first + 2])

    def pair_down(value, first, buffer, copies, own, store):
        value = value.astype(BF)
        for i in (0, 1):
            inc = value[:, 256 * i : 256 * i + 256]
            child = (store[i] - nt(inc, fcou[first + i].reshape(512, 256))).astype(BF)
            for j in (0, 1):
                buffer[2 * i + j] = child[:, 256 * j : 256 * j + 256]
            for t in range(4 * i, 4 * i + 4):
                if t != own:
                    copies[t][0].start()

    @pl.when(top)
    def _():
        for place in (5, 6):
            passed[0, place][1].wait_recv()
            passed[1, place][1].wait_recv()
        wait_factors(0, 7)

    @pl.when(spine)
    def _():
        for place in (2, 3, 4):
            passed[0, place][1].wait_recv()
            passed[1, place][1].wait_recv()
        solved = pair_up(up34, u34, 2, fsv)
        cs[2] = squeeze(solved, fbas[4])
        fsv[2] = solved
        begin(up5[0], z % 2 == 0)

        @pl.when(z_odd)
        def _():
            wait_factors(0, 1)
            wait_factors(1, 1)
            up5[1].wait_recv()
            solved = solve(u5[...], cs[2], finv[1])
            cs[3] = squeeze(solved, fbas[1])
            for m in range(4):
                begin(up67[m][0], z == 2 * m + 1)
            rounded = solved.astype(BF)
            sb5[...] = rounded[:, :256]
            sh5[...] = rounded[:, 256:]
            share5[0].start()

    point(7)
    own_c3 = local(ncou.at[6], c3h.at[x % 2])
    own_c3.start()
    send_c3 = remote(ncou.at[6], c3h.at[x % 2], at(z, y, core, xs[1]), my_dst=c3h.at[xs[1] % 2])
    send_c3[0].start()
    c2_sem = counter[0]
    counter[0] += 4
    c2_away = []
    for m in (0, 1):
        target = 2 * m + x // 2
        copy = pltpu.make_async_remote_copy(
            src_ref=ncou.at[4 + m], dst_ref=c2h.at[x % 2], send_sem=ssem.at[c2_sem + m],
            recv_sem=rsem.at[c2_sem + x % 2], device_id=at(z, y, core, target), device_id_type=MESH,
        )
        away = target != x
        pending.append((away, copy))
        c2_away.append((copy, away))
        begin(copy, away)
    own_c2 = local(ncou.at[4 + x // 2], c2h.at[x % 2])
    own_c2_here = (x == 0) | (x == 3)
    begin(own_c2, own_c2_here)

    @pl.when(top)
    def _():
        solved = pair_up(up67, u67, 5, fsz)
        passed[2, 5][1].wait_recv()
        passed[2, 6][1].wait_recv()
        pair_down(solved, 5, vz, down_z, 4, fsz)
        id5[...] = vz[2]

    @pl.when(spine)
    def _():
        for place in (2, 3, 4):
            passed[2, place][1].wait_recv()
        half = 2 * (z % 2)
        for j in (0, 1):
            wait_factor(2, 9, half + j)

        @pl.when(z != 4)
        def _():
            down_z[0][1].wait_recv()

        @pl.when(z % 2 == 0)
        def _():
            share5[1].wait_recv()

        rows = fcou[9, pl.ds(half, 2)].reshape(256, 256)
        inc = (sh5[...].astype(F32) - nt(id5[...], rows)).astype(BF)
        value = fsv[2] - nt(inc, fcou[4].reshape(512, 256))
        pair_down(value, 2, vy, down_y, -1, fsv)

    @pl.when(plane)
    def _():
        wait_factors(2, 0)
        half = 2 * (y % 2)
        for j in (0, 1):
            wait_factor(2, 8, half + j)

        down_y[0][1].wait_recv()
        share2[0][1].wait_recv()

        rows = fcou[8, pl.ds(half, 2)].reshape(256, 256)
        inc = (sh2[...].astype(F32) - nt(id2[...], rows)).astype(BF)
        value = (fs1[...] - nt(inc, fcou[0].reshape(512, 256))).astype(BF)
        vcore[...] = value[:, :256]
        cross_down[0].start()
        inc3[...] = value[:, 256:]

    @pl.when(is0 & home)
    def _():
        cross_down[1].wait_recv()

    landing = counter[0]
    inc_in = {
        t: remote(inc3, inc3, at(z, y, core, t), cond=home, lands=landing) for t in (0, 2, 3)
    }
    for t in (0, 2, 3):
        begin(inc_in[t][0], home)

    for _, recv in move_c1:
        recv.wait_recv()
    own_n1[2].wait()
    own_c3.wait()
    send_c3[1].wait_recv()
    from_x = 2 * (x % 2)
    for j in (0, 1):
        @pl.when(from_x + j != x)
        def _(j=j):
            pltpu.make_async_remote_copy(
                src_ref=ncou.at[4], dst_ref=c2h.at[j], send_sem=ssem.at[c2_sem],
                recv_sem=rsem.at[c2_sem + j], device_id=at(z, y, core, xs[1]), device_id_type=MESH,
            ).wait_recv()

    @pl.when(own_c2_here)
    def _():
        own_c2.wait()

    @pl.when(x_odd)
    def _():
        share_s2[1].wait_recv()

    @pl.when(jnp.logical_not(home))
    def _():
        share_s3[0][1].wait_recv()
        inc_in[0][1].wait_recv()

    value = (s3h[...].astype(F32) - nt(inc3[...], c3h[...].reshape(256, 256))).astype(BF)
    value = (s2h[...].astype(F32) - nt(value, c2h[...].reshape(256, 256))).astype(BF)
    value = (s1[...] - nt(value, n1c[...].reshape(512, 256))).astype(BF)
    i0[x, 0] = value[:, :256]
    i0[x, 1] = value[:, 256:]
    spread = {
        k: remote(i0.at[x], i0.at[x], at(z, y, core, xs[k]), my_dst=i0.at[xs[k]]) for k in ALONG_X
    }
    for k in ALONG_X:
        spread[k][0].start()
    own_lcou.wait()
    for k in (0, 1, 3, 2):
        if k:
            spread[k][1].wait_recv()
        for j in range(2):
            l = 2 * xs[k] + j
            out[l] = lv[l] - nt(i0[xs[k], j], lcou_v[l])

    def left(copy, cond):
        if cond is None:
            copy.wait_send()
        else:
            @pl.when(cond)
            def _():
                copy.wait_send()

    for cond, copy in pending:
        left(copy, cond)
    left(factor_copy(0), has_inv)
    left(factor_copy(1), has_rest)
    left(factor_copy(2), has_rest)


def body(rs, po, linv, lbas, lcou, ninv, nbas, ncou):
    vm = pl.BlockSpec(memory_space=pltpu.VMEM)
    hbm = pl.BlockSpec(memory_space=pl.ANY)
    dma = pltpu.SemaphoreType.DMA
    part = VMEM((64, 256), BF)
    scratch = [
        VMEM((3, 64, 1024), BF), VMEM((64, 4096), F32), VMEM((8, 64, 128), F32),
        VMEM((8, 128, 512), BF), VMEM((8, 128, 256), BF), VMEM((8, 128, 256), BF),
        VMEM((4, 2, 64, 256), BF), VMEM((3, 2, 64, 256), BF),
        VMEM((4, 128, 512), BF), VMEM((4, 128, 256), BF), VMEM((4, 128, 256), BF),
        VMEM((4, 128, 512), BF), VMEM((4, 128, 256), BF),
        VMEM((2, 128, 256), BF), VMEM((2, 128, 256), BF),
        VMEM((64, 512), F32), VMEM((2, 64, 256), BF), VMEM((2, 64, 256), BF), part, part,
        part, part, part, VMEM((2, 64, 256), BF),
        VMEM((8, 4, 128, 512), BF), VMEM((8, 4, 128, 256), BF), VMEM((10, 4, 128, 256), BF),
        VMEM((64, 512), F32), VMEM((3, 64, 512), F32), VMEM((2, 64, 512), F32), VMEM((4, 64, 256), BF),
        part, VMEM((2, 64, 256), BF), VMEM((4, 64, 256), BF), part, VMEM((4, 64, 256), BF),
        part, part, VMEM((2, 64, 256), BF), part, part, part, VMEM((4, 64, 256), BF), VMEM((4, 64, 256), BF),
        part, part, VMEM((4, 2, 64, 256), BF),
        dma((12,)), dma((N_SEMS,)), dma((N_SEMS,)), dma((3,)), dma((3, 10, 4)),
    ]
    return pl.pallas_call(
        kernel,
        out_shape=jax.ShapeDtypeStruct((8, 64, 128), F32),
        in_specs=[vm, vm] + [hbm] * 6,
        out_specs=vm,
        scratch_shapes=scratch,
        compiler_params=pltpu.CompilerParams(
            collective_id=0, has_side_effects=True, vmem_limit_bytes=60 << 20
        ),
    )(rs, po.reshape(1, 4096), linv, lbas, lcou, ninv, nbas, ncou)


def solution(mesh):
    placed = (
        P(None, ("leaf", "rhs")),
        P("leaf"),
        P("leaf", "rhs", None),
        P("leaf", "rhs", None),
        P("leaf", "rhs", None),
        P("leaf", "rhs", None),
        P("leaf", "rhs", None),
        P("leaf", "rhs", None),
    )
    return jax.shard_map(
        body, mesh=mesh, in_specs=placed, out_specs=P("leaf", None, "rhs"), check_vma=False
    )
```

```python
import jax
import jax.numpy as jnp
from jax import lax
from jax.experimental import pallas as pl
from jax.experimental.pallas import tpu as pltpu
from jax.sharding import PartitionSpec as P

MESH = pl.DeviceIdType.MESH
BF = jnp.bfloat16
F32 = jnp.float32
VMEM = pltpu.VMEM
HOME = 1
HIGH = 2
N_SEMS = 128
ALONG_X = (1, 3, 2)
WHEN = {0: (), 1: ("fi", "fb", "n1i", "n1b"), 2: (), 3: (), 4: (), 5: ("n2",), 6: ("pi", "pb", "n3"), 7: ("fc", "c1", "pc")}


def nt(a, b):
    return lax.dot_general(a, b, (((1,), (1,)), ((), ())), preferred_element_type=F32)


def nn(a, b):
    return lax.dot_general(a, b, (((1,), (0,)), ((), ())), preferred_element_type=F32)


def xor(a, k):
    total = 0
    for bit in (1, 2):
        digit = (a // bit) % 2
        total = total + bit * ((1 - digit) if k & bit else digit)
    return total


def as_int(cond):
    return jnp.where(cond, 1, 0)


def kernel(
    rs, po, linv, lbas, lcou, ninv, nbas, ncou, out,
    tg, spots, acc, lv, linv_v, lbas_v, lcou_v, rsb, rsr,
    n1i, n1b, n1c, n2i, n2b, c2h, c3h,
    s1, s2b, s3b, s2h, s3h, cb1, u2x, cb2, u3x,
    finv, fbas, fcou, fs1, fsv, fsz, cs, u1, u2, u34, u5, u67,
    sh2, sh5, sb2, sb5, id2, id5, vy, vz, vcore, inc3, i0,
    lsem, ssem, rsem, fss, frs,
):
    leaf = lax.axis_index("leaf")
    x = lax.axis_index("rhs")
    core = leaf % 2
    y = (leaf // 2) % 8
    z = leaf // 16

    def at(z_, y_, c_, x_):
        return ((z_ * 8 + y_) * 2 + c_, x_)

    counter = [0]
    pending = []

    def remote(src, dst, target, my_dst=None, cond=None, lands=None):
        i = counter[0]
        counter[0] += 1
        j = i if lands is None else lands
        made = [
            pltpu.make_async_remote_copy(
                src_ref=src, dst_ref=here, send_sem=ssem.at[i], recv_sem=rsem.at[j],
                device_id=target, device_id_type=MESH,
            )
            for here in (dst, dst if my_dst is None else my_dst)
        ]
        pending.append((cond, made[0]))
        return made

    def begin(copy, cond=None):
        if cond is None:
            copy.start()
        else:
            @pl.when(cond)
            def _():
                copy.start()

    local_count = [0]

    def local(src, dst):
        i = local_count[0]
        local_count[0] += 1
        return pltpu.make_async_copy(src, dst, lsem.at[i])

    xs = [xor(x, k) for k in range(4)]
    is0 = core == 0
    is1 = core == 1
    y_odd = y % 2 == 1
    z_odd = z % 2 == 1
    y_pair = y + 1 - 2 * (y % 2)
    z_pair = z + 1 - 2 * (z % 2)
    home = x == HOME
    plane = is1 & home
    high = is1 & (x == HIGH)
    spine = high & (y == 0)
    top = spine & (z == 4)
    low = x < 2

    own_linv, own_lbas, own_lcou = (
        local(linv, linv_v), local(lbas, lbas_v), local(lcou, lcou_v)
    )
    own_n1 = [local(a.at[x], b.at[x]) for a, b in ((ninv, n1i), (nbas, n1b), (ncou, n1c))]
    for copy in [own_linv, own_lbas, own_lcou] + own_n1:
        copy.start()

    def entry(at_x):
        return 4 + as_int(at_x == 1) * 2 + as_int(at_x == 2)

    has_n2 = x != 3
    own_entry = jnp.where(has_n2, entry(x), 4)
    own_n2 = [local(a.at[own_entry], b.at[x]) for a, b in ((ninv, n2i), (nbas, n2b))]
    for copy in own_n2:
        copy.start()

    barrier = pltpu.get_barrier_semaphore()

    def greet(*target):
        pl.semaphore_signal(barrier, inc=1, device_id=at(*target), device_id_type=MESH)

    def greet_if(cond, *targets):
        @pl.when(cond)
        def _():
            for target in targets:
                greet(*target)

    for k in ALONG_X:
        greet(z, y, core, xs[k])
    greet(z, y, 1 - core, x)
    odds = (1, 3, 5, 7)
    y_even = y % 2 == 0
    z_even = z % 2 == 0
    greet_if(plane & y_odd, *[(z, y, 0, r) for r in (2, 3)])
    greet_if(plane & y_even, *[(z, y + 1, 0, r) for r in (0, 1)])
    greet_if(plane, (z, y + as_int(y_even), 1, HIGH), (z, 0, 1, HIGH))
    greet_if(high & y_odd, *[(z, y, 0, r) for r in range(4)])
    greet_if(high & y_odd, (z, y, 1, HOME), (z, y - 1, 1, HOME))
    greet_if(high & y_even & (y > 0), *[(z, y, 0, r) for r in range(4)])
    greet_if(spine, *[(z, t, 1, HIGH) for t in range(1, 8)])
    greet_if(spine, (z_pair, 0, 1, HIGH))
    greet_if(spine & (z > 0), *[(z, 0, 0, r) for r in range(4)])
    greet_if(spine & z_even, *[(z + 1, 0, 0, r) for r in (0, 1)])
    greet_if(spine & (z != 4), (4, 0, 1, HIGH))
    greet_if(top, *[(t, 0, 1, HIGH) for t in (1, 2, 3, 5, 6, 7)])
    mover = jnp.where(y > 0, 1 + as_int(y_odd), as_int(z > 0) + as_int(z_odd & low))
    expect = (
        4
        + as_int(is0) * mover
        + as_int(plane)
        + as_int(high & y_odd) * 3
        + as_int(high & y_even & (y > 0))
        + as_int(spine) * (9 + as_int(z_odd) + as_int(z % 4 == 2))
        + as_int(top) * 7
    )
    pl.semaphore_wait(barrier, expect)

    gather = {k: remote(rs, tg.at[k - 1], at(z, y, core, xs[k])) for k in ALONG_X}
    gather[1][0].start()
    gather[3][0].start()
    gather[2][0].start()

    def along_x(src, dst, k, cond=None):
        return remote(src, dst.at[x], at(z, y, core, xs[k]), my_dst=dst.at[xs[k]], cond=cond)

    move_n1 = [along_x(a.at[xs[k]], b, k) for a, b in ((ninv, n1i), (nbas, n1b)) for k in ALONG_X]
    move_c1 = [along_x(ncou.at[xs[k]], n1c, k) for k in ALONG_X]
    goes_n2 = {k: xs[k] != 3 for k in ALONG_X}
    move_n2 = [
        along_x(a.at[jnp.where(goes_n2[k], entry(xs[k]), 4)], b, k, cond=goes_n2[k])
        for a, b in ((ninv, n2i), (nbas, n2b))
        for k in ALONG_X
    ]

    first_row = is0 & (y == 0)
    slot = jnp.where(
        is1,
        0,
        jnp.where(
            y > 0,
            jnp.where(y_odd, 1, jnp.where(y == 2, 2, jnp.where(y == 6, 3, 4))),
            jnp.where(z_odd, 1, jnp.where(z == 2, 5, jnp.where(z == 6, 6, 7))),
        ),
    )
    halved_y = is0 & y_odd
    halved_z = first_row & z_odd
    slot_c = jnp.where(halved_y, 8, jnp.where(halved_z, 9, slot))
    to_y_c = y - as_int(halved_y & low)
    to_z_c = z - as_int(halved_z & low)
    stays = plane
    to_x = jnp.where(is1, HOME, HIGH)
    to_x_c = jnp.where(halved_y, HOME, to_x)
    has_inv = jnp.logical_not(first_row & (z == 0)) & jnp.logical_not(stays)
    has_rest = has_inv & jnp.logical_not(first_row & (z == 4))
    factors = ((ninv.at[7], finv), (nbas.at[7], fbas), (ncou.at[7], fcou))

    def factor_copy(which):
        src, dst = factors[which]
        place = slot_c if which == 2 else slot
        target = at(to_z_c, to_y_c, 1, to_x_c) if which == 2 else at(z, y, 1, to_x)
        return pltpu.make_async_remote_copy(
            src_ref=src, dst_ref=dst.at[place, x], send_sem=fss.at[which],
            recv_sem=frs.at[which, place, x], device_id=target, device_id_type=MESH,
        )

    def factor_own(which):
        src, dst = factors[which]
        return pltpu.make_async_copy(src, dst.at[0, HOME], fss.at[which])

    def send_factors(which):
        begin(factor_copy(which), has_inv if which == 0 else has_rest)
        begin(factor_own(which), stays)

    def wait_factor(which, place, r):
        src, dst = factors[which]
        pltpu.make_async_remote_copy(
            src_ref=src, dst_ref=dst.at[place, r], send_sem=fss.at[which],
            recv_sem=frs.at[which, place, r], device_id=at(z, y, 0, x), device_id_type=MESH,
        ).wait_recv()

    def wait_factors(which, place):
        for r in range(4):
            if place == 0 and r == HOME:
                factor_own(which).wait()
            else:
                wait_factor(which, place, r)

    def start_all(moves, conds=None):
        for n, (send, _) in enumerate(moves):
            begin(send, conds[n] if conds else None)

    level2_conds = [xs[k] % 2 == 0 for k in ALONG_X] * 2
    level3_conds = [xs[k] == HOME for k in ALONG_X] * 2
    items = {
        "n1i": lambda: start_all(move_n1[:3]),
        "n1b": lambda: start_all(move_n1[3:]),
        "n2": lambda: start_all(move_n2, level2_conds),
        "n3": lambda: start_all(move_n2, level3_conds),
        "fi": lambda: send_factors(0),
        "fb": lambda: send_factors(1),
        "fc": lambda: send_factors(2),
        "c1": lambda: start_all(move_c1),
        "pi": lambda: pass_on(0),
        "pb": lambda: pass_on(1),
        "pc": lambda: pass_on(2),
    }

    def point(n):
        for item in WHEN[n]:
            items[item]()

    passing = [(2, high & (y == 2), (z, 0)), (3, high & (y == 6), (z, 0)), (4, high & (y == 4), (z, 0))]
    passing += [(5, spine & (z == 2), (4, 0)), (6, spine & (z == 6), (4, 0))]
    passed = {
        (which, place): remote(
            factors[which][1].at[place], factors[which][1].at[place], at(*to, 1, HIGH), cond=cond
        )
        for place, cond, to in passing
        for which in range(3)
    }

    def pass_on(which):
        for place, cond, _ in passing:
            @pl.when(cond)
            def _(place=place):
                wait_factors(which, place)
                passed[which, place][0].start()

    def find_spots(j, carry):
        cols = pl.ds(pl.multiple_of(j * 512, 512), 512)
        rows = lax.broadcasted_iota(jnp.int32, (256, 512), 0)
        spots[:, cols] = jnp.where(rows == po[:, cols] % 256, 1.0, 0.0).astype(BF)
        return carry

    lax.fori_loop(0, 8, find_spots, 0)

    def permute(block, source, first):
        group = po[...] // 256 - source * 4
        stacked = jnp.concatenate([block[:, 256 * g : 256 * g + 256] for g in range(4)], axis=0)
        candidates = nn(stacked, spots[...])
        value = jnp.zeros((64, 4096), F32) if first else acc[...]
        for g in range(4):
            value = jnp.where(group == g, candidates[64 * g : 64 * g + 64], value)
        acc[...] = value

    point(0)
    permute(rs[...], x, True)
    point(1)
    gather[1][1].wait_recv()
    permute(tg[0], xs[1], False)
    point(2)
    gather[3][1].wait_recv()
    permute(tg[2], xs[3], False)
    point(3)
    gather[2][1].wait_recv()
    permute(tg[1], xs[2], False)

    own_linv.wait()
    own_lbas.wait()
    scatter = {k: remote(rsb.at[xs[k]], rsr.at[k - 1], at(z, y, core, xs[k])) for k in ALONG_X}
    for k in (2, 1, 3, 0):
        for j in range(2):
            l = 2 * xs[k] + j
            cols = pl.ds(pl.multiple_of(l * 512, 512), 512)
            value = nt(acc[:, cols].astype(BF), linv_v[l])
            lv[l] = value
            rsb[xs[k], j] = nn(value.astype(BF), lbas_v[l]).astype(BF)
        if k:
            scatter[k][0].start()
    point(4)
    for k in ALONG_X:
        scatter[k][1].wait_recv()

    def summed(j):
        total = rsb[x, j].astype(F32)
        for k in range(3):
            total = total + rsr[k, j].astype(F32)
        return total.astype(BF)

    def solve(left, right, inverse):
        return nt(jnp.concatenate([left, right], axis=1), inverse.reshape(512, 512))

    def squeeze(solved, basis):
        return nn(solved.astype(BF), basis.reshape(512, 256)).astype(BF)

    point(5)
    for _, recv in move_n1:
        recv.wait_recv()
    own_n1[0].wait()
    own_n1[1].wait()
    solved = solve(summed(0), summed(1), n1i[...])
    s1[...] = solved
    cb1[...] = squeeze(solved, n1b[...])

    x_odd = x % 2 == 1
    x_even = x % 2 == 0
    up_l1 = remote(cb1, u2x, at(z, y, core, xs[1]), cond=x_odd)
    to_home = counter[0]
    up_l2 = [
        remote(cb2, u3x.at[i], at(z, y, core, HOME), cond=x == 2 * i) for i in (0, 1)
    ]
    share_s2 = remote(s2b.at[1], s2h, at(z, y, core, xs[1]), cond=x_even)
    landing = counter[0]
    share_s3 = {
        t: remote(s3b.at[t // 2], s3h, at(z, y, core, t), cond=home, lands=landing) for t in (0, 2, 3)
    }
    begin(up_l1[0], x_odd)
    point(6)

    own_n2[0].wait()
    own_n2[1].wait()

    @pl.when(has_n2)
    def _():
        for _, recv in move_n2:
            recv.wait_recv()

    @pl.when(x_even)
    def _():
        up_l1[1].wait_recv()
        solved = solve(cb1[...], u2x[...], n2i[...])
        cb2[...] = squeeze(solved, n2b[...])
        for i in (0, 1):
            begin(up_l2[i][0], x == 2 * i)
        rounded = solved.astype(BF)
        s2b[1] = rounded[:, 256:]
        s2h[...] = rounded[:, :256]
        share_s2[0].start()

    @pl.when(home)
    def _():
        for i in (0, 1):
            up_l2[i][1].wait_recv()
        solved = solve(u3x[0], u3x[1], n2i[...])
        cb2[...] = squeeze(solved, n2b[...])
        rounded = solved.astype(BF)
        s3b[0] = rounded[:, :256]
        s3b[1] = rounded[:, 256:]

    cross_up = remote(cb2, u1, at(z, y, 1, x), cond=is0 & home)
    begin(cross_up[0], is0 & home)
    for t in (0, 2, 3):
        begin(share_s3[t][0], home)

    @pl.when(home)
    def _():
        s3h[...] = s3b[HOME // 2]

    high_odd = high & y_odd
    spine_odd = spine & z_odd
    spine_even = spine & z_even
    y_own = y + as_int(y_even)
    up2 = [
        remote(cs.at[0], u2.at[i], at(z, y_own, 1, HIGH), cond=plane & (y % 2 == i)) for i in (0, 1)
    ]
    landing = counter[0]
    share2 = [
        remote(sb2.at[i], sh2, at(z, y - 1 + i, 1, HOME), cond=high_odd, lands=landing) for i in (0, 1)
    ]
    up34 = [
        remote(cs.at[1], u34.at[m], at(z, 0, 1, x), cond=high & (y == 2 * m + 1)) for m in range(4)
    ]
    up5 = remote(cs.at[2], u5, at(z_pair, 0, 1, x), cond=spine_even)
    share5 = remote(sb5, sh5, at(z_pair, 0, 1, x), cond=spine_odd)
    up67 = [
        remote(cs.at[3], u67.at[m], at(4, 0, 1, x), cond=spine & (z == 2 * m + 1)) for m in range(4)
    ]
    landing = counter[0]
    down_z = {
        t: remote(vz.at[t // 2], id5, at(t, 0, 1, x), cond=top, lands=landing)
        for t in (0, 1, 2, 3, 5, 6, 7)
    }
    landing = counter[0]
    down_y = {
        t: remote(vy.at[t // 2], id2, at(z, t, 1, HOME), cond=spine, lands=landing) for t in range(8)
    }
    cross_down = remote(vcore, inc3, at(z, y, 0, x), cond=plane)

    @pl.when(plane)
    def _():
        wait_factors(0, 0)
        wait_factors(1, 0)
        cross_up[1].wait_recv()
        solved = solve(u1[...], cb2[...], finv[0])
        cs[0] = squeeze(solved, fbas[0])
        for i in (0, 1):
            begin(up2[i][0], y % 2 == i)
        fs1[...] = solved

    @pl.when(high_odd)
    def _():
        wait_factors(0, 1)
        wait_factors(1, 1)
        for i in (0, 1):
            up2[i][1].wait_recv()
        solved = solve(u2[0], u2[1], finv[1])
        cs[1] = squeeze(solved, fbas[1])
        for m in range(4):
            begin(up34[m][0], y == 2 * m + 1)
        rounded = solved.astype(BF)
        for i in (0, 1):
            sb2[i] = rounded[:, 256 * i : 256 * i + 256]
            share2[i][0].start()

    def pair_up(arrived, buffer, first, store):
        squeezed = []
        for i in (0, 1):
            arrived[2 * i][1].wait_recv()
            arrived[2 * i + 1][1].wait_recv()
            solved = solve(buffer[2 * i], buffer[2 * i + 1], finv[first + i])
            store[i] = solved
            squeezed.append(squeeze(solved, fbas[first + i]))
        return solve(squeezed[0], squeezed[1], finv[first + 2])

    def pair_down(value, first, buffer, copies, own, store):
        value = value.astype(BF)
        for i in (0, 1):
            inc = value[:, 256 * i : 256 * i + 256]
            child = (store[i] - nt(inc, fcou[first + i].reshape(512, 256))).astype(BF)
            for j in (0, 1):
                buffer[2 * i + j] = child[:, 256 * j : 256 * j + 256]
            for t in range(4 * i, 4 * i + 4):
                if t != own:
                    copies[t][0].start()

    @pl.when(top)
    def _():
        for place in (5, 6):
            passed[0, place][1].wait_recv()
            passed[1, place][1].wait_recv()
        wait_factors(0, 7)

    @pl.when(spine)
    def _():
        for place in (2, 3, 4):
            passed[0, place][1].wait_recv()
            passed[1, place][1].wait_recv()
        solved = pair_up(up34, u34, 2, fsv)
        cs[2] = squeeze(solved, fbas[4])
        fsv[2] = solved
        begin(up5[0], z % 2 == 0)

        @pl.when(z_odd)
        def _():
            wait_factors(0, 1)
            wait_factors(1, 1)
            up5[1].wait_recv()
            solved = solve(u5[...], cs[2], finv[1])
            cs[3] = squeeze(solved, fbas[1])
            for m in range(4):
                begin(up67[m][0], z == 2 * m + 1)
            rounded = solved.astype(BF)
            sb5[...] = rounded[:, :256]
            sh5[...] = rounded[:, 256:]
            share5[0].start()

    point(7)
    own_c3 = local(ncou.at[6], c3h.at[x % 2])
    own_c3.start()
    send_c3 = remote(ncou.at[6], c3h.at[x % 2], at(z, y, core, xs[1]), my_dst=c3h.at[xs[1] % 2])
    send_c3[0].start()
    c2_sem = counter[0]
    counter[0] += 4
    c2_away = []
    for m in (0, 1):
        target = 2 * m + x // 2
        copy = pltpu.make_async_remote_copy(
            src_ref=ncou.at[4 + m], dst_ref=c2h.at[x % 2], send_sem=ssem.at[c2_sem + m],
            recv_sem=rsem.at[c2_sem + x % 2], device_id=at(z, y, core, target), device_id_type=MESH,
        )
        away = target != x
        pending.append((away, copy))
        c2_away.append((copy, away))
        begin(copy, away)
    own_c2 = local(ncou.at[4 + x // 2], c2h.at[x % 2])
    own_c2_here = (x == 0) | (x == 3)
    begin(own_c2, own_c2_here)

    @pl.when(top)
    def _():
        solved = pair_up(up67, u67, 5, fsz)
        passed[2, 5][1].wait_recv()
        passed[2, 6][1].wait_recv()
        pair_down(solved, 5, vz, down_z, 4, fsz)
        id5[...] = vz[2]

    @pl.when(spine)
    def _():
        for place in (2, 3, 4):
            passed[2, place][1].wait_recv()
        half = 2 * (z % 2)
        for j in (0, 1):
            wait_factor(2, 9, half + j)

        @pl.when(z != 4)
        def _():
            down_z[0][1].wait_recv()

        @pl.when(z % 2 == 0)
        def _():
            share5[1].wait_recv()

        rows = fcou[9, pl.ds(half, 2)].reshape(256, 256)
        inc = (sh5[...].astype(F32) - nt(id5[...], rows)).astype(BF)
        value = fsv[2] - nt(inc, fcou[4].reshape(512, 256))
        pair_down(value, 2, vy, down_y, -1, fsv)

    @pl.when(plane)
    def _():
        wait_factors(2, 0)
        half = 2 * (y % 2)
        for j in (0, 1):
            wait_factor(2, 8, half + j)

        down_y[0][1].wait_recv()
        share2[0][1].wait_recv()

        rows = fcou[8, pl.ds(half, 2)].reshape(256, 256)
        inc = (sh2[...].astype(F32) - nt(id2[...], rows)).astype(BF)
        value = (fs1[...] - nt(inc, fcou[0].reshape(512, 256))).astype(BF)
        vcore[...] = value[:, :256]
        cross_down[0].start()
        inc3[...] = value[:, 256:]

    @pl.when(is0 & home)
    def _():
        cross_down[1].wait_recv()

    landing = counter[0]
    inc_in = {
        t: remote(inc3, inc3, at(z, y, core, t), cond=home, lands=landing) for t in (0, 2, 3)
    }
    for t in (0, 2, 3):
        begin(inc_in[t][0], home)

    for _, recv in move_c1:
        recv.wait_recv()
    own_n1[2].wait()
    own_c3.wait()
    send_c3[1].wait_recv()
    from_x = 2 * (x % 2)
    for j in (0, 1):
        @pl.when(from_x + j != x)
        def _(j=j):
            pltpu.make_async_remote_copy(
                src_ref=ncou.at[4], dst_ref=c2h.at[j], send_sem=ssem.at[c2_sem],
                recv_sem=rsem.at[c2_sem + j], device_id=at(z, y, core, xs[1]), device_id_type=MESH,
            ).wait_recv()

    @pl.when(own_c2_here)
    def _():
        own_c2.wait()

    @pl.when(x_odd)
    def _():
        share_s2[1].wait_recv()

    @pl.when(jnp.logical_not(home))
    def _():
        share_s3[0][1].wait_recv()
        inc_in[0][1].wait_recv()

    value = (s3h[...].astype(F32) - nt(inc3[...], c3h[...].reshape(256, 256))).astype(BF)
    value = (s2h[...].astype(F32) - nt(value, c2h[...].reshape(256, 256))).astype(BF)
    value = (s1[...] - nt(value, n1c[...].reshape(512, 256))).astype(BF)
    i0[x, 0] = value[:, :256]
    i0[x, 1] = value[:, 256:]
    spread = {
        k: remote(i0.at[x], i0.at[x], at(z, y, core, xs[k]), my_dst=i0.at[xs[k]]) for k in ALONG_X
    }
    for k in ALONG_X:
        spread[k][0].start()
    own_lcou.wait()
    for k in (0, 1, 3, 2):
        if k:
            spread[k][1].wait_recv()
        for j in range(2):
            l = 2 * xs[k] + j
            out[l] = lv[l] - nt(i0[xs[k], j], lcou_v[l])

    def left(copy, cond):
        if cond is None:
            copy.wait_send()
        else:
            @pl.when(cond)
            def _():
                copy.wait_send()

    for cond, copy in pending:
        left(copy, cond)
    left(factor_copy(0), has_inv)
    left(factor_copy(1), has_rest)
    left(factor_copy(2), has_rest)


def body(rs, po, linv, lbas, lcou, ninv, nbas, ncou):
    vm = pl.BlockSpec(memory_space=pltpu.VMEM)
    hbm = pl.BlockSpec(memory_space=pl.ANY)
    dma = pltpu.SemaphoreType.DMA
    part = VMEM((64, 256), BF)
    scratch = [
        VMEM((3, 64, 1024), BF), VMEM((256, 4096), BF), VMEM((64, 4096), F32), VMEM((8, 64, 128), F32),
        VMEM((8, 128, 512), BF), VMEM((8, 128, 256), BF), VMEM((8, 128, 256), BF),
        VMEM((4, 2, 64, 256), BF), VMEM((3, 2, 64, 256), BF),
        VMEM((4, 128, 512), BF), VMEM((4, 128, 256), BF), VMEM((4, 128, 256), BF),
        VMEM((4, 128, 512), BF), VMEM((4, 128, 256), BF),
        VMEM((2, 128, 256), BF), VMEM((2, 128, 256), BF),
        VMEM((64, 512), F32), VMEM((2, 64, 256), BF), VMEM((2, 64, 256), BF), part, part,
        part, part, part, VMEM((2, 64, 256), BF),
        VMEM((8, 4, 128, 512), BF), VMEM((8, 4, 128, 256), BF), VMEM((10, 4, 128, 256), BF),
        VMEM((64, 512), F32), VMEM((3, 64, 512), F32), VMEM((2, 64, 512), F32), VMEM((4, 64, 256), BF),
        part, VMEM((2, 64, 256), BF), VMEM((4, 64, 256), BF), part, VMEM((4, 64, 256), BF),
        part, part, VMEM((2, 64, 256), BF), part, part, part, VMEM((4, 64, 256), BF), VMEM((4, 64, 256), BF),
        part, part, VMEM((4, 2, 64, 256), BF),
        dma((12,)), dma((N_SEMS,)), dma((N_SEMS,)), dma((3,)), dma((3, 10, 4)),
    ]
    return pl.pallas_call(
        kernel,
        out_shape=jax.ShapeDtypeStruct((8, 64, 128), F32),
        in_specs=[vm, vm] + [hbm] * 6,
        out_specs=vm,
        scratch_shapes=scratch,
        compiler_params=pltpu.CompilerParams(
            collective_id=0, has_side_effects=True, vmem_limit_bytes=60 << 20
        ),
    )(rs, po.reshape(1, 4096), linv, lbas, lcou, ninv, nbas, ncou)


def solution(mesh):
    placed = (
        P(None, ("leaf", "rhs")),
        P("leaf"),
        P("leaf", "rhs", None),
        P("leaf", "rhs", None),
        P("leaf", "rhs", None),
        P("leaf", "rhs", None),
        P("leaf", "rhs", None),
        P("leaf", "rhs", None),
    )
    return jax.shard_map(
        body, mesh=mesh, in_specs=placed, out_specs=P("leaf", None, "rhs"), check_vma=False
    )
```
